256 devices in a mesh: dp: 128 (over z, y, x_lo, core), rep: 2 (over x_hi).
Axes of the slice: x: 4 (x_hi: 2, x_lo: 2; x = x_hi * 2 + x_lo), y: 4, z: 8, core: 2. Of those that a mesh axis runs over, the one named last changes fastest.
Arguments:
- picture_vectors: bfloat16 [65536, 1152], P('dp'), may hold values from -1 to 1
- caption_vectors: bfloat16 [65536, 1152], P('dp'), may hold values from -1 to 1
- matched_caption_index: int32 [128, 512], P('dp'), may hold values from 0 to 511, as said below
- score_multiplier: float32 [], replicated, may hold values from 90 to 110
- score_offset: float32 [], replicated, may hold values from -10.5 to -9.5
- objective_cotangent: float32 [], replicated, may hold values from 0.1 to 0.3
Outputs:
- picture_vector_derivative: float32 [65536, 1152], P('dp')
- caption_vector_derivative: float32 [65536, 1152], P('dp')
The draws below stay inside these ranges and needn't reach their ends.
Inputs may be any that keep to these rules, and one draw needn't show every extreme that they name: Each row matched_caption_index[p] is a permutation of 0 .. 511.
All inputs are finite; a program needn't handle non-finite values.
Results may differ from the reference program's by a relative error of at most 0.0045.
Values may be sent and summed in bfloat16 or wider, within the bound.
A program may use at most 64 MiB of HBM per device.

```python
import jax
import jax.numpy as jnp
from jax import lax

FEATURE_DIM = 1152
COUPLES_PER_PART = 512
STEPS = 8
N_DP = 128


def pairing(key):
    keys = jax.random.split(jax.random.fold_in(key, 11), N_DP)
    return jax.vmap(lambda single: jax.random.permutation(single, COUPLES_PER_PART))(keys).astype(jnp.int32)


def embeddings(key):
    factor = (FEATURE_DIM * 1152.0) ** (-0.25)
    base = jax.random.normal(jax.random.fold_in(key, 21), (N_DP, COUPLES_PER_PART, FEATURE_DIM), jnp.float32) * factor
    return jnp.clip(base, -1.0, 1.0)


def draw_matched_caption_index(key, part):
    pairs = pairing(key)
    return pairs


def draw_picture_vectors(key, part):
    vectors = embeddings(key)
    return vectors.reshape(N_DP * COUPLES_PER_PART, FEATURE_DIM).astype(jnp.bfloat16)


def draw_caption_vectors(key, part):
    vectors = embeddings(key)
    pairs = pairing(key)
    key = jax.random.fold_in(key, 9)
    factor = (FEATURE_DIM * 1152.0) ** (-0.25)
    cosine = jax.random.uniform(jax.random.fold_in(key, 1), (N_DP, COUPLES_PER_PART, 1), jnp.float32, 0.1, 0.4)
    noise = jax.random.normal(jax.random.fold_in(key, 2), (N_DP, COUPLES_PER_PART, FEATURE_DIM), jnp.float32) * factor
    paired = cosine * vectors + jnp.sqrt(1.0 - cosine * cosine) * noise
    placed = jax.vmap(lambda block, order: jnp.zeros_like(block).at[order].set(block))(paired, pairs)
    return jnp.clip(placed, -1.0, 1.0).reshape(N_DP * COUPLES_PER_PART, FEATURE_DIM).astype(jnp.bfloat16)


def setup_inputs(seed: int = 0) -> dict:
    key_list = jax.random.split(jax.random.key(seed), 7)
    return {
        "picture_vectors": draw_picture_vectors(jax.random.fold_in(key_list[6], 71), 0),
        "caption_vectors": draw_caption_vectors(jax.random.fold_in(key_list[6], 71), 0),
        "matched_caption_index": draw_matched_caption_index(jax.random.fold_in(key_list[6], 71), 0),
        "score_multiplier": jnp.clip(jax.random.uniform(key_list[3], (), jnp.float32, 90.0, 110.0), 90.0, 110.0),
        "score_offset": jnp.clip(jax.random.uniform(key_list[4], (), jnp.float32, -10.5, -9.5), -10.5, -9.5),
        "objective_cotangent": jnp.clip(jax.random.uniform(key_list[5], (), jnp.float32, 0.1, 0.3), 0.1, 0.3),
    }


def reference(picture_vectors, caption_vectors, matched_caption_index, score_multiplier, score_offset, objective_cotangent):
    img = picture_vectors.reshape(N_DP, COUPLES_PER_PART, FEATURE_DIM).astype(jnp.float32)
    txt = caption_vectors.reshape(N_DP, COUPLES_PER_PART, FEATURE_DIM).astype(jnp.float32)
    column = lax.broadcasted_iota(jnp.int32, (N_DP, COUPLES_PER_PART, COUPLES_PER_PART), 2)
    match = (column == matched_caption_index[:, :, None]).astype(jnp.float32)
    picture_derivative_piece = jnp.zeros((N_DP, COUPLES_PER_PART, FEATURE_DIM), jnp.float32)
    caption_derivative_piece = jnp.zeros((N_DP, COUPLES_PER_PART, FEATURE_DIM), jnp.float32)
    for step in range(STEPS):
        moved = jnp.roll(txt, step, axis=0)
        inner_score_table = jnp.einsum('prd,pqd->prq', img, moved)
        couple_score_table = score_multiplier * inner_score_table + score_offset
        positive = 1.0 if step == 0 else 0.0
        grads = (objective_cotangent * (jax.nn.sigmoid(couple_score_table) - positive * match)).astype(jnp.bfloat16)
        grads_wide = grads.astype(jnp.float32)
        picture_derivative_piece = picture_derivative_piece + jnp.einsum('prq,pqd->prd', grads_wide, moved)
        contrib = jnp.einsum('prq,prd->pqd', grads_wide, img)
        caption_derivative_piece = caption_derivative_piece + jnp.roll(contrib, -step, axis=0)
    picture_vector_derivative = (score_multiplier * picture_derivative_piece).reshape(N_DP * COUPLES_PER_PART, FEATURE_DIM)
    caption_vector_derivative = (score_multiplier * caption_derivative_piece).reshape(N_DP * COUPLES_PER_PART, FEATURE_DIM)
    return picture_vector_derivative, caption_vector_derivative
```

```python
import functools

import jax
import jax.numpy as jnp
from jax import lax
from jax.experimental import pallas as pl
from jax.experimental.pallas import tpu as pltpu
from jax.sharding import PartitionSpec as P

MESH = pl.DeviceIdType.MESH
PIECES = 4

NAMES = (
    "sib", "b1_0", "b1_1", "a2_0", "a2_1", "b2_0", "b2_1", "a1_0", "a1_1",
    "b3_0", "b3_1", "a3_0", "a3_1", "a4", "b4",
)
SLOT = {name: i for i, name in enumerate(NAMES)}

FORWARD = (
    {
        "a2_0": lambda j: [("X", "b3_1"), ("S", "a2_0")] if j < 2 else [("S", "a2_0")],
        "b1_0": lambda j: [("S", "b1_0")],
        "b2_0": lambda j: [("X", "a1_1"), ("P", "b4"), ("S", "b2_0")],
        "a1_0": lambda j: [("N", "a3_0"), ("S", "a1_0")],
        "b3_0": lambda j: [("S", "b3_0")],
        "b4": lambda j: [("X", "a3_1"), ("S", "b4")],
        "a3_0": lambda j: [("S", "a3_0")],
    },
    {
        "a2_1": lambda j: [("X", "b3_0"), ("N0", "a4"), ("S", "a2_1")],
        "b1_1": lambda j: [("P", "b3_1"), ("S", "b1_1")] if j >= 2 else [("S", "b1_1")],
        "b2_1": lambda j: [("X", "a1_0"), ("S", "b2_1")],
        "a1_1": lambda j: [("S", "a1_1")],
        "b3_1": lambda j: [("X", "a2_0"), ("S", "b3_1")] if j >= 2 else [("S", "b3_1")],
        "a3_1": lambda j: [("S", "a3_1")],
    },
)

PLAN = (
    [
        "b2_0:0", "a2_0:0", "b1_0:0", "b1_0:1", "b2_0:1", "a2_0:1", "b1_0:2", "b1_0:3", "T.b1_0",
        "T.b1_1",
        "b2_0:2", "a1_0:0", "a1_0:1", "T.a2_1",
        "b2_0:3", "T.b2_0",
        "b3_0:0", "b3_0:1", "T.b2_1",
        "a1_0:2", "b4:0", "a1_0:3", "T.a1_0",
        "b3_0:2", "b3_0:3", "T.b3_0",
        "b4:1", "T.a1_1",
        "a3_0:0", "b4:2", "T.a4",
        "a3_0:1", "a2_0:2", "a2_0:3", "T.b3_1",
        "T.a2_0",
        "b4:3", "a3_0:2", "H.a3_0.0",
        "a3_0:3", "H.a3_0.1",
        "H.a3_1.0",
        "H.a3_1.1",
    ],
    [
        "b2_1:0", "a2_1:0", "b1_1:0", "b1_1:1", "b2_1:1", "a2_1:1", "b1_1:2", "b1_1:3", "T.b1_1",
        "T.b1_0",
        "a2_1:2", "b2_1:2", "a2_1:3", "T.a2_1",
        "a1_1:0", "a1_1:1", "b2_1:3", "T.b2_1",
        "b3_1:0", "b3_1:1", "T.b2_0",
        "b3_1:2", "a1_1:2", "a1_1:3", "T.a1_1",
        "b3_1:3", "T.b3_0",
        "T.a1_0",
        "T.b3_1",
        "T.a2_0",
        "a3_1:0", "a3_1:1", "T.b4",
        "H.a3_0.0",
        "a3_1:2", "a3_1:3", "H.a3_0.1",
        "H.a3_1.0",
        "H.a3_1.1",
    ],
)


def coordinates():
    shard, replica = lax.axis_index("dp"), lax.axis_index("rep")
    return shard // 16, (shard // 4) % 4, replica * 2 + (shard // 2) % 2, shard % 2


def device(z, y, x, core):
    return (z * 16 + y * 4 + (x % 2) * 2 + core, x // 2)


def kernel(
    rows, scalars, match_ref, picture_hbm, caption_hbm, picture_out, caption_out,
    own, held, total, load_sem, send_sem, recv_sem, store_sem,
):
    z, y, x, core = coordinates()
    kind = x % 2
    logical = (core + kind) % 2
    part = rows // PIECES
    up = ((z + (y + 1) // 4) % 8, (y + 1) % 4)
    down = ((z + 7 + (y + 3) // 4) % 8, (y + 3) % 4)
    next_z, next_y = [u * (1 - kind) + d * kind for u, d in zip(up, down)]
    prev_z, prev_y = [d * (1 - kind) + u * kind for u, d in zip(up, down)]
    place = {
        "S": device(z, y, x, 1 - core),
        "N": device(next_z, next_y, x, core),
        "P": device(prev_z, prev_y, x, core),
        "N0": device(next_z, next_y, x, kind),
        "P1": device(prev_z, prev_y, x, 1 - kind),
        "R": device(z, y, (x + 1) % 4, core),
        "L": device(z, y, (x + 3) % 4, core),
    }

    loads = [
        pltpu.make_async_copy(picture_hbm, own.at[1 - kind], load_sem.at[0]),
        pltpu.make_async_copy(caption_hbm, own.at[kind], load_sem.at[1]),
    ]
    for load in loads:
        load.start()

    barrier = pltpu.get_barrier_semaphore()
    for where in "SNPRL":
        pl.semaphore_signal(barrier, inc=1, device_id=place[where], device_id_type=MESH)

    @pl.when(logical == 0)
    def _():
        pl.semaphore_signal(barrier, inc=1, device_id=place["P1"], device_id_type=MESH)
        pl.semaphore_wait(barrier, 5)

    @pl.when(logical == 1)
    def _():
        pl.semaphore_wait(barrier, 6)

    for load in loads:
        load.wait()

    sent = ([], [])

    def piece(ref, block, j, count=1):
        return ref.at[block, pl.ds(j * part, count * part)]

    def send(c, src, where, name, j, count=1):
        if where == "X":
            where = "RL"[j % 2]
        index = len(sent[c])

        def copy():
            return pltpu.make_async_remote_copy(
                src_ref=piece(src[0], src[1], j, count),
                dst_ref=piece(held, SLOT[name], j, count),
                send_sem=send_sem.at[index],
                recv_sem=recv_sem.at[SLOT[name], j],
                device_id=place[where],
                device_id_type=MESH,
            )

        copy().start()
        sent[c].append(copy)

    def arrived(name, j, count=1):
        here = piece(held, SLOT[name], j, count)
        pltpu.make_async_remote_copy(
            src_ref=here, dst_ref=here, send_sem=send_sem.at[0], recv_sem=recv_sem.at[SLOT[name], j],
            device_id=place["S"], device_id_type=MESH,
        ).wait_recv()

    for c in (0, 1):

        @pl.when(logical == c)
        def _(c=c):
            send(c, (own, c), "S", "sib", 0, PIECES)
            for j in range(PIECES):
                if c == 1 or j < 2:
                    send(c, (own, 0), "N", "a2_%d" % c, j)
                send(c, (own, 1), "P", "b2_%d" % c, j)
                send(c, (own, 0), "X", "b1_%d" % (1 - c), j)

    multiplier, offset, cotangent = scalars[0], scalars[1], scalars[2]
    slope, shift = -multiplier, -offset

    def gradient(left, right):
        table = lax.dot_general(left, right, (((1,), (1,)), ((), ())), preferred_element_type=jnp.float32)
        return cotangent / (1.0 + jnp.exp(slope * table + shift))

    row = lax.broadcasted_iota(jnp.int32, (rows, rows), 0)
    paired = (row == match_ref[...]).astype(jnp.float32)
    turned = paired.T
    is_a = (kind == 0).astype(jnp.float32)
    positive = is_a * turned + (1.0 - is_a) * paired
    first = (gradient(own[1], own[0]) - cotangent * positive).astype(jnp.bfloat16)
    total[0] = jnp.dot(first, own[0], preferred_element_type=jnp.float32)
    total[1] = lax.dot_general(first, own[1], (((0,), (0,)), ((), ())), preferred_element_type=jnp.float32)

    half = rows // 2

    def work(which, block, start, size):
        @pl.loop(0, rows, step=half)
        def _(r):
            here = pl.ds(pl.multiple_of(r, half), half)
            other = held[block, pl.ds(start, size)]
            grads = gradient(own[1 - which, here], other).astype(jnp.bfloat16)
            total[which, here] += jnp.dot(grads, other, preferred_element_type=jnp.float32)

    def pick(values):
        return values[0] if values[0] == values[1] else values[0] * (1 - logical) + values[1] * logical

    arrived("sib", 0, PIECES)
    work(1 - logical, SLOT["sib"], 0, rows)

    position = [0, 0]
    waited = [set(), set()]
    while position[0] < len(PLAN[0]):
        step = []
        for c in (0, 1):
            events = []
            while PLAN[c][position[c]][1] != ".":
                events.append(PLAN[c][position[c]])
                position[c] += 1
            task = PLAN[c][position[c]].split(".")
            position[c] += 1
            step.append(task)

            @pl.when(logical == c)
            def _(c=c, events=events, task=task):
                for event in events:
                    name, j = event.split(":")
                    j = int(j)
                    arrived(name, j)
                    waited[c].add((name, j))
                    for where, target in FORWARD[c][name](j):
                        send(c, (held, SLOT[name]), where, target, j)
                pieces = range(PIECES) if task[0] == "T" else range(2 * int(task[2]), 2 * int(task[2]) + 2)
                for j in pieces:
                    if (task[1], j) not in waited[c]:
                        assert task[1] not in FORWARD[c]
                        arrived(task[1], j)
                        waited[c].add((task[1], j))

        block = pick([SLOT[task[1]] for task in step])
        which = pick([0 if task[1][0] == "a" else 1 for task in step])
        if step[0][0] == "T":
            work(which, block, 0, rows)
        else:
            work(which, block, half * int(step[0][2]), half)

    for c in (0, 1):

        @pl.when(logical == c)
        def _(c=c):
            for name in NAMES:
                for j in range(PIECES):
                    assert (name, j) in waited[c] or name in ("sib", "a4" if c else "")
            for copy in sent[c]:
                copy().wait_send()

    total[...] = total[...] * multiplier
    for value in (0, 1):

        @pl.when(kind == value)
        def _(value=value):
            stores = [
                pltpu.make_async_copy(total.at[value], picture_out, store_sem.at[0]),
                pltpu.make_async_copy(total.at[1 - value], caption_out, store_sem.at[1]),
            ]
            for store in stores:
                store.start()
            for store in stores:
                store.wait()


def per_device(pictures, captions, matched, multiplier, offset, cotangent):
    rows, width = pictures.shape
    scalars = jnp.stack([multiplier, offset, cotangent])
    out = jax.ShapeDtypeStruct((rows, width), jnp.float32)
    return pl.pallas_call(
        functools.partial(kernel, rows),
        out_shape=(out, out),
        in_specs=[
            pl.BlockSpec(memory_space=pltpu.SMEM),
            pl.BlockSpec(memory_space=pltpu.VMEM),
            pl.BlockSpec(memory_space=pl.ANY),
            pl.BlockSpec(memory_space=pl.ANY),
        ],
        out_specs=(pl.BlockSpec(memory_space=pl.ANY), pl.BlockSpec(memory_space=pl.ANY)),
        scratch_shapes=[
            pltpu.VMEM((2, rows, width), jnp.bfloat16),
            pltpu.VMEM((len(NAMES), rows, width), jnp.bfloat16),
            pltpu.VMEM((2, rows, width), jnp.float32),
            pltpu.SemaphoreType.DMA((2,)),
            pltpu.SemaphoreType.DMA((80,)),
            pltpu.SemaphoreType.DMA((len(NAMES), PIECES)),
            pltpu.SemaphoreType.DMA((2,)),
        ],
        compiler_params=pltpu.CompilerParams(
            collective_id=0, has_side_effects=True, vmem_limit_bytes=52 * 2**20
        ),
        cost_estimate=pl.CostEstimate(
            flops=31 * 2 * rows * rows * width, bytes_accessed=12 * rows * width, transcendentals=16 * rows * rows
        ),
        name="band",
    )(scalars, matched, pictures, captions)


def solution(mesh):
    placed = (P("dp", None), P("dp", None), P("dp", None), P(), P(), P())
    return jax.shard_map(
        per_device,
        mesh=mesh,
        in_specs=placed,
        out_specs=(P("dp", None), P("dp", None)),
        check_vma=False,
    )
```

```python
import functools

import jax
import jax.numpy as jnp
from jax import lax
from jax.experimental import pallas as pl
from jax.experimental.pallas import tpu as pltpu
from jax.sharding import PartitionSpec as P

MESH = pl.DeviceIdType.MESH
PIECES = 4
SPLIT = 3
LIMIT = 36

NAMES = (
    "sib", "b1_0", "b1_1", "a2_0", "a2_1", "b2_0", "b2_1", "a1_0", "a1_1",
    "b3_0", "b3_1", "a3_0", "a3_1", "a4", "b4",
)
SLOT = {name: i for i, name in enumerate(NAMES)}

FORWARD = (
    {
        "a2_0": lambda j: [("X", "b3_1"), ("S", "a2_0")] if j < SPLIT else [("S", "a2_0")],
        "b1_0": lambda j: [("S", "b1_0")],
        "b2_0": lambda j: [("X", "a1_1"), ("P", "b4"), ("S", "b2_0")],
        "a1_0": lambda j: [("N", "a3_0"), ("S", "a1_0")],
        "b3_0": lambda j: [("S", "b3_0")],
        "b4": lambda j: [("X", "a3_1"), ("S", "b4")],
        "a3_0": lambda j: [("S", "a3_0")],
    },
    {
        "a2_1": lambda j: [("X", "b3_0"), ("N0", "a4"), ("S", "a2_1")],
        "b1_1": lambda j: [("P", "b3_1"), ("S", "b1_1")] if j >= SPLIT else [("S", "b1_1")],
        "b2_1": lambda j: [("X", "a1_0"), ("S", "b2_1")],
        "a1_1": lambda j: [("S", "a1_1")],
        "b3_1": lambda j: [("X", "a2_0"), ("S", "b3_1")] if j >= SPLIT else [("S", "b3_1")],
        "a3_1": lambda j: [("S", "a3_1")],
    },
)

OWN = (
    [
        "P.b2_0:0", "X.b1_1:3", "P.b2_0:1", "X.b1_1:0", "N.a2_0:1", "P.b2_0:2", "N.a2_0:2", "X.b1_1:2",
        "N.a2_0:0", "X.b1_1:1", "P.b2_0:3",
    ],
    [
        "N.a2_1:2", "P.b2_1:3", "X.b1_0:0", "P.b2_1:2", "P.b2_1:0", "N.a2_1:3", "P.b2_1:1", "X.b1_0:3",
        "N.a2_1:1", "X.b1_0:2", "X.b1_0:1", "N.a2_1:0",
    ],
)

PLAN = (
    [
        "b2_0:0", "a2_0:1", "a2_0:2", "b2_0:1", "H.b1_1.1",
        "H.b1_1.0",
        "b2_0:2", "a2_0:0", "a1_0:3", "b1_0:3", "b1_0:1", "b1_0:0", "b1_0:2", "T.b1_0",
        "b2_0:3", "H.a2_0.0",
        "b3_0:2", "H.b2_1.1",
        "H.a2_1.1",
        "b3_0:3", "H.b3_0.1",
        "H.a2_1.0",
        "a1_0:2", "T.b2_0",
        "b3_0:1", "b4:0", "T.b3_1",
        "b4:1", "a1_0:1", "a1_0:0", "H.b2_1.0",
        "b4:2", "T.a1_0",
        "a3_0:3", "a2_0:3", "a3_0:2", "b4:3", "b3_0:0", "T.a1_1",
        "T.a4",
        "H.b3_0.0",
        "H.a2_0.1",
        "a3_0:1", "a3_0:0", "T.a3_0",
        "T.a3_1",
    ],
    [
        "b1_1:0", "b1_1:3", "b1_1:2", "b2_1:3", "a1_1:0", "b1_1:1", "a2_1:2", "H.b1_1.0",
        "a2_1:3", "H.a2_0.0",
        "b3_1:2", "b3_1:1", "a2_1:1", "H.b1_1.1",
        "b2_1:1", "b2_1:2", "a2_1:0", "T.a2_1",
        "b2_1:0", "T.b2_0",
        "b3_1:0", "b3_1:3", "T.b3_1",
        "a1_1:3", "T.b2_1",
        "T.b1_0",
        "a1_1:1", "H.a1_1.0",
        "a1_1:2", "H.a1_1.1",
        "T.a1_0",
        "H.a2_0.1",
        "T.b4",
        "a3_1:0", "T.b3_0",
        "a3_1:2", "a3_1:1", "a3_1:3", "T.a3_1",
        "T.a3_0",
    ],
)


def coordinates():
    shard, replica = lax.axis_index("dp"), lax.axis_index("rep")
    return shard // 16, (shard // 4) % 4, replica * 2 + (shard // 2) % 2, shard % 2


def device(z, y, x, core):
    return (z * 16 + y * 4 + (x % 2) * 2 + core, x // 2)


def kernel(
    rows, scalars, match_hbm, picture_hbm, caption_hbm, total,
    own, held, match_ref, load_sem, send_sem, recv_sem,
):
    z, y, x, core = coordinates()
    kind = x % 2
    logical = (core + kind) % 2
    part = rows // PIECES
    up = ((z + (y + 1) // 4) % 8, (y + 1) % 4)
    down = ((z + 7 + (y + 3) // 4) % 8, (y + 3) % 4)
    next_z, next_y = [u * (1 - kind) + d * kind for u, d in zip(up, down)]
    prev_z, prev_y = [d * (1 - kind) + u * kind for u, d in zip(up, down)]
    place = {
        "S": device(z, y, x, 1 - core),
        "N": device(next_z, next_y, x, core),
        "P": device(prev_z, prev_y, x, core),
        "N0": device(next_z, next_y, x, kind),
        "P1": device(prev_z, prev_y, x, 1 - kind),
        "R": device(z, y, (x + 1) % 4, core),
        "L": device(z, y, (x + 3) % 4, core),
    }

    loads = [
        pltpu.make_async_copy(picture_hbm, own.at[1 - kind], load_sem.at[0]),
        pltpu.make_async_copy(caption_hbm, own.at[kind], load_sem.at[1]),
        pltpu.make_async_copy(match_hbm, match_ref, load_sem.at[2]),
    ]
    for load in loads:
        load.start()

    barrier = pltpu.get_barrier_semaphore()
    for where in "SNPRL":
        pl.semaphore_signal(barrier, inc=1, device_id=place[where], device_id_type=MESH)

    @pl.when(logical == 0)
    def _():
        pl.semaphore_signal(barrier, inc=1, device_id=place["P1"], device_id_type=MESH)
        pl.semaphore_wait(barrier, 5)

    @pl.when(logical == 1)
    def _():
        pl.semaphore_wait(barrier, 6)

    for load in loads:
        load.wait()

    sent = ([], [])

    def piece(ref, block, j, count=1):
        return ref.at[block, pl.ds(j * part, count * part)]

    def send(c, src, where, name, j, count=1):
        if where == "X":
            where = "RL"[j % 2]
        index = len(sent[c])

        def copy():
            return pltpu.make_async_remote_copy(
                src_ref=piece(src[0], src[1], j, count),
                dst_ref=piece(held, SLOT[name], j, count),
                send_sem=send_sem.at[index],
                recv_sem=recv_sem.at[SLOT[name], j],
                device_id=place[where],
                device_id_type=MESH,
            )

        copy().start()
        sent[c].append(copy)

    def arrived(name, j, count=1):
        here = piece(held, SLOT[name], j, count)
        pltpu.make_async_remote_copy(
            src_ref=here, dst_ref=here, send_sem=send_sem.at[0], recv_sem=recv_sem.at[SLOT[name], j],
            device_id=place["S"], device_id_type=MESH,
        ).wait_recv()

    for c in (0, 1):

        @pl.when(logical == c)
        def _(c=c):
            send(c, (own, c), "S", "sib", 0, PIECES)
            for item in OWN[c]:
                where, target = item.split(".")
                name, j = target.split(":")
                send(c, (own, 1 if where == "P" else 0), where, name, int(j))

    multiplier, offset, cotangent = scalars[0], scalars[1], scalars[2]
    slope, shift = -multiplier, -offset

    def gradient(left, right):
        table = lax.dot_general(left, right, (((1,), (1,)), ((), ())), preferred_element_type=jnp.float32)
        return cotangent / (1.0 + jnp.exp(slope * table + shift))

    row = lax.broadcasted_iota(jnp.int32, (rows, rows), 0)
    paired = (row == match_ref[...]).astype(jnp.float32)
    turned = paired.T
    is_a = (kind == 0).astype(jnp.float32)
    positive = is_a * turned + (1.0 - is_a) * paired
    first = (gradient(own[1], own[0]) - cotangent * positive).astype(jnp.bfloat16)
    total[kind] = jnp.dot(first, own[0], preferred_element_type=jnp.float32)
    total[1 - kind] = lax.dot_general(first, own[1], (((0,), (0,)), ((), ())), preferred_element_type=jnp.float32)

    half = rows // 2

    def work(which, block, start, size):
        other = held[block, pl.ds(start, size)]
        grads = gradient(own[1 - which], other).astype(jnp.bfloat16)
        output = which * (1 - kind) + (1 - which) * kind
        total[output] += jnp.dot(grads, other, preferred_element_type=jnp.float32)

    arrived("sib", 0, PIECES)
    work(1 - logical, SLOT["sib"], 0, rows)

    steps = []
    for c in (0, 1):
        waited, list_c, events = set(), [], []
        for item in PLAN[c]:
            if ":" in item:
                name, j = item.split(":")
                events.append((name, int(j), FORWARD[c][name](int(j))))
                waited.add((name, int(j)))
                continue
            task = item.split(".")
            start = 0 if task[0] == "T" else 2 * int(task[2])
            for j in range(start, start + (PIECES if task[0] == "T" else 2)):
                if (task[1], j) not in waited:
                    assert task[1] not in FORWARD[c]
                    events.append((task[1], j, []))
                    waited.add((task[1], j))
            list_c.append((events, task[0] == "T", SLOT[task[1]], 0 if task[1][0] == "a" else 1, start))
            events = []
        missing = {(name, j) for name in NAMES for j in range(PIECES)} - waited
        assert not events and {name for name, _ in missing} == {"sib", "b4" if c == 0 else "a4"} - {n for n, _ in waited}
        steps.append(list_c)
    count = max(len(list_c) for list_c in steps)

    def lookup(k, field, default):
        values = []
        for list_c in steps:
            value = jnp.int32(default)
            for n in range(len(list_c)):
                value = jnp.where(k == n, int(list_c[n][field]), value)
            values.append(value)
        return jnp.where(logical == 0, values[0], values[1])

    def branch(k, low, high, run):
        if high - low == 1:
            run(low)
            return
        middle = (low + high) // 2

        @pl.when(k < middle)
        def _():
            branch(k, low, middle, run)

        @pl.when(k >= middle)
        def _():
            branch(k, middle, high, run)

    def take(c, n):
        for name, j, targets in steps[c][n][0]:
            arrived(name, j)
            for where, target in targets:
                send(c, (held, SLOT[name]), where, target, j)

    @pl.loop(0, count)
    def _(k):
        for c in (0, 1):

            @pl.when((logical == c) & (k < len(steps[c])))
            def _(c=c):
                branch(k, 0, len(steps[c]), functools.partial(take, c))

        full = lookup(k, 1, 2)
        block = lookup(k, 2, 0)
        which = lookup(k, 3, 0)
        start = lookup(k, 4, 0) * part

        @pl.when(full == 1)
        def _():
            work(which, block, 0, rows)

        @pl.when(full == 0)
        def _():
            work(which, block, pl.multiple_of(start, half), half)

    for c in (0, 1):

        @pl.when(logical == c)
        def _(c=c):
            for copy in sent[c]:
                copy().wait_send()


def per_device(pictures, captions, matched, multiplier, offset, cotangent):
    rows, width = pictures.shape
    scalars = jnp.stack([multiplier, offset, cotangent])
    matched, pictures, captions = (pltpu.with_memory_space_constraint(v, pltpu.HBM) for v in (matched, pictures, captions))
    sums = pl.pallas_call(
        functools.partial(kernel, rows),
        out_shape=jax.ShapeDtypeStruct((2, rows, width), jnp.float32),
        in_specs=[
            pl.BlockSpec(memory_space=pltpu.SMEM),
            pl.BlockSpec(memory_space=pltpu.HBM),
            pl.BlockSpec(memory_space=pltpu.HBM),
            pl.BlockSpec(memory_space=pltpu.HBM),
        ],
        out_specs=pl.BlockSpec(memory_space=pltpu.VMEM),
        scratch_shapes=[
            pltpu.VMEM((2, rows, width), jnp.bfloat16),
            pltpu.VMEM((len(NAMES), rows, width), jnp.bfloat16),
            pltpu.VMEM((1, rows), jnp.int32),
            pltpu.SemaphoreType.DMA((3,)),
            pltpu.SemaphoreType.DMA((80,)),
            pltpu.SemaphoreType.DMA((len(NAMES), PIECES)),
        ],
        compiler_params=pltpu.CompilerParams(
            collective_id=0, has_side_effects=True, vmem_limit_bytes=LIMIT * 2**20
        ),
        cost_estimate=pl.CostEstimate(
            flops=31 * 2 * rows * rows * width, bytes_accessed=12 * rows * width, transcendentals=16 * rows * rows
        ),
        name="band",
    )(scalars, matched, pictures, captions)
    return multiplier * sums[0], multiplier * sums[1]


def solution(mesh):
    placed = (P("dp", None), P("dp", None), P("dp", None), P(), P(), P())
    return jax.shard_map(
        per_device,
        mesh=mesh,
        in_specs=placed,
        out_specs=(P("dp", None), P("dp", None)),
        check_vma=False,
    )
```

```python
import functools

import jax
import jax.numpy as jnp
from jax import lax
from jax.experimental import pallas as pl
from jax.experimental.pallas import tpu as pltpu
from jax.sharding import PartitionSpec as P

MESH = pl.DeviceIdType.MESH
PIECES = 8
SPLIT = 5
LIMIT = 36

NAMES = (
    "sib", "b1_0", "b1_1", "a2_0", "a2_1", "b2_0", "b2_1", "a1_0", "a1_1",
    "b3_0", "b3_1", "a3_0", "a3_1", "a4", "b4",
)
SLOT = {name: i for i, name in enumerate(NAMES)}

FORWARD = (
    {
        "a2_0": lambda j: [("X", "b3_1"), ("S", "a2_0")] if j < SPLIT else [("S", "a2_0")],
        "b1_0": lambda j: [("S", "b1_0")],
        "b2_0": lambda j: [("X", "a1_1"), ("P", "b4"), ("S", "b2_0")],
        "a1_0": lambda j: [("N", "a3_0"), ("S", "a1_0")],
        "b3_0": lambda j: [("S", "b3_0")],
        "b4": lambda j: [("X", "a3_1"), ("S", "b4")],
        "a3_0": lambda j: [("S", "a3_0")],
    },
    {
        "a2_1": lambda j: [("X", "b3_0"), ("N0", "a4"), ("S", "a2_1")],
        "b1_1": lambda j: [("P", "b3_1"), ("S", "b1_1")] if j >= SPLIT else [("S", "b1_1")],
        "b2_1": lambda j: [("X", "a1_0"), ("S", "b2_1")],
        "a1_1": lambda j: [("S", "a1_1")],
        "b3_1": lambda j: [("X", "a2_0"), ("S", "b3_1")] if j >= SPLIT else [("S", "b3_1")],
        "a3_1": lambda j: [("S", "a3_1")],
    },
)

sib, b1_0, b1_1, a2_0, a2_1, b2_0, b2_1, a1_0, a1_1, b3_0, b3_1, a3_0, a3_1, a4, b4 = NAMES
T, H, D, SEND, N, P_, X = "T", "H", "D", ">", "N", "P", "X"

OWN = (
    [
        (N, a2_0, 0), (X, b1_1, 4), (X, b1_1, 6), (X, b1_1, 7), (P_, b2_0, 0), (P_, b2_0, 3), (X, b1_1, 1),
        (X, b1_1, 3), (N, a2_0, 2),
    ],
    [
        (P_, b2_1, 3), (X, b1_0, 6), (P_, b2_1, 4), (N, a2_1, 4),
    ],
)

PLAN = (
    [
        (SEND, P_, b2_0, 4), (SEND, X, b1_1, 2), (SEND, X, b1_1, 0), (SEND, X, b1_1, 5), (SEND, P_, b2_0, 5),
        (SEND, N, a2_0, 4), (SEND, N, a2_0, 1), (SEND, P_, b2_0, 6), (b1_0, 0), (a2_0, 0), (SEND, P_, b2_0, 1),
        (b1_0, 6), (SEND, N, a2_0, 3), (SEND, P_, b2_0, 7), (a2_0, 1), (b1_0, 4), (a1_0, 3), (SEND, P_, b2_0, 2),
        (T, b1_1),
        (b1_0, 5), (b1_0, 7), (H, b1_0, 1),
        (b3_0, 6), (b1_0, 3), (a2_0, 2), (b3_0, 0), (a1_0, 1), (H, a2_1, 0),
        (a2_0, 4), (b1_0, 2), (a1_0, 4), (b2_0, 4), (b2_0, 0), (b2_0, 1), (b2_0, 2), (b2_0, 3),
        (D, a2_1, 1, b2_0, 0),
        (b2_0, 5), (b2_0, 6), (b2_0, 7), (H, b2_0, 1),
        (b3_0, 1), (b3_0, 2), (b3_0, 3), (b3_0, 4), (b3_0, 5), (b3_0, 7), (T, b3_0),
        (b1_0, 1), (a2_0, 3), (T, b2_1),
        (a1_0, 2), (a1_0, 0), (b4, 0), (H, b1_0, 0),
        (a1_0, 5), (a1_0, 6), (a1_0, 7), (T, a1_0),
        (H, b3_1, 1),
        (b4, 1), (H, b3_1, 0),
        (b4, 2), (b4, 5), (b4, 3), (a2_0, 7), (b4, 4), (a2_0, 6), (a3_0, 1), (a2_0, 5), (T, a2_0),
        (a3_0, 4), (b4, 6), (a3_0, 0), (b4, 7), (a3_0, 2), (T, a1_1),
        (a3_0, 5), (a3_0, 3), (D, a4, 1, a3_0, 0),
        (a3_0, 6), (a3_0, 7), (D, a4, 0, a3_0, 1),
        (T, a3_1),
    ],
    [
        (SEND, X, b1_0, 0), (SEND, X, b1_0, 7), (SEND, P_, b2_1, 5), (SEND, N, a2_1, 3), (SEND, X, b1_0, 4),
        (SEND, X, b1_0, 1), (b1_1, 3), (SEND, N, a2_1, 1), (SEND, P_, b2_1, 2), (SEND, N, a2_1, 6),
        (SEND, X, b1_0, 3), (SEND, N, a2_1, 0), (SEND, N, a2_1, 5), (SEND, P_, b2_1, 1), (b1_1, 4),
        (SEND, X, b1_0, 2), (SEND, P_, b2_1, 6), (SEND, X, b1_0, 5), (SEND, P_, b2_1, 0), (b2_1, 5), (b1_1, 6),
        (b2_1, 2), (SEND, P_, b2_1, 7), (b1_1, 0), (b1_1, 5), (SEND, N, a2_1, 2), (b2_1, 4), (SEND, N, a2_1, 7),
        (b1_1, 7), (b2_1, 3), (a2_1, 6), (b1_1, 1), (b1_1, 2), (H, b1_1, 0),
        (H, b1_1, 1),
        (b2_1, 1), (a2_1, 1), (a2_1, 0), (a2_1, 2), (a2_1, 3), (a2_1, 4), (a2_1, 5), (a2_1, 7), (T, a2_1),
        (b2_1, 0), (b2_1, 6), (b2_1, 7), (T, b2_1),
        (T, b2_0),
        (H, b1_0, 0),
        (H, b1_0, 1),
        (a1_1, 0), (b3_1, 6), (b3_1, 4), (b3_1, 2), (b3_1, 5), (b3_1, 7), (D, b3_1, 1, b3_0, 0),
        (a1_1, 3), (b3_1, 0), (b3_1, 1), (b3_1, 3), (D, b3_1, 0, b3_0, 1),
        (a1_1, 1), (a1_1, 2), (a1_1, 4), (a1_1, 5), (a1_1, 6), (a1_1, 7), (T, a1_1),
        (T, a1_0),
        (T, a2_0),
        (T, b4),
        (a3_1, 2), (a3_1, 6), (a3_1, 5), (a3_1, 0), (a3_1, 1), (a3_1, 3), (a3_1, 4), (a3_1, 7), (T, a3_1),
        (T, a3_0),
    ],
)


def coordinates():
    shard, replica = lax.axis_index("dp"), lax.axis_index("rep")
    return shard // 16, (shard // 4) % 4, replica * 2 + (shard // 2) % 2, shard % 2


def device(z, y, x, core):
    return (z * 16 + y * 4 + (x % 2) * 2 + core, x // 2)


def kernel(
    rows, scalars, match_hbm, picture_hbm, caption_hbm, total,
    own, held, match_ref, load_sem, send_sem, recv_sem,
):
    z, y, x, core = coordinates()
    kind = x % 2
    logical = (core + kind) % 2
    part = rows // PIECES
    up = ((z + (y + 1) // 4) % 8, (y + 1) % 4)
    down = ((z + 7 + (y + 3) // 4) % 8, (y + 3) % 4)
    next_z, next_y = [u * (1 - kind) + d * kind for u, d in zip(up, down)]
    prev_z, prev_y = [d * (1 - kind) + u * kind for u, d in zip(up, down)]
    place = {
        "S": device(z, y, x, 1 - core),
        "N": device(next_z, next_y, x, core),
        "P": device(prev_z, prev_y, x, core),
        "N0": device(next_z, next_y, x, kind),
        "P1": device(prev_z, prev_y, x, 1 - kind),
        "R": device(z, y, (x + 1) % 4, core),
        "L": device(z, y, (x + 3) % 4, core),
    }

    loads = [
        pltpu.make_async_copy(picture_hbm, own.at[1 - kind], load_sem.at[0]),
        pltpu.make_async_copy(caption_hbm, own.at[kind], load_sem.at[1]),
        pltpu.make_async_copy(match_hbm, match_ref, load_sem.at[2]),
    ]
    for load in loads:
        load.start()

    barrier = pltpu.get_barrier_semaphore()
    for where in "SNPRL":
        pl.semaphore_signal(barrier, inc=1, device_id=place[where], device_id_type=MESH)

    @pl.when(logical == 0)
    def _():
        pl.semaphore_signal(barrier, inc=1, device_id=place["P1"], device_id_type=MESH)
        pl.semaphore_wait(barrier, 5)

    @pl.when(logical == 1)
    def _():
        pl.semaphore_wait(barrier, 6)

    for load in loads:
        load.wait()

    sent = ([], [])

    def piece(ref, block, j, count=1):
        return ref.at[block, pl.ds(j * part, count * part)]

    def send(c, src, where, name, j, count=1):
        if where == "X":
            where = "RL"[j % 2]
        index = len(sent[c])

        def copy():
            return pltpu.make_async_remote_copy(
                src_ref=piece(src[0], src[1], j, count),
                dst_ref=piece(held, SLOT[name], j, count),
                send_sem=send_sem.at[index],
                recv_sem=recv_sem.at[SLOT[name], j],
                device_id=place[where],
                device_id_type=MESH,
            )

        copy().start()
        sent[c].append(copy)

    def arrived(name, j, count=1):
        here = piece(held, SLOT[name], j, count)
        pltpu.make_async_remote_copy(
            src_ref=here, dst_ref=here, send_sem=send_sem.at[0], recv_sem=recv_sem.at[SLOT[name], j],
            device_id=place["S"], device_id_type=MESH,
        ).wait_recv()

    def send_own(c, item):
        where, name, j = item
        send(c, (own, 1 if where == "P" else 0), where, name, j)

    for c in (0, 1):

        @pl.when(logical == c)
        def _(c=c):
            send(c, (own, c), "S", "sib", 0, PIECES)
            for item in OWN[c]:
                send_own(c, item)

    multiplier, offset, cotangent = scalars[0], scalars[1], scalars[2]
    slope, shift = -multiplier, -offset

    def gradient(left, right):
        table = lax.dot_general(left, right, (((1,), (1,)), ((), ())), preferred_element_type=jnp.float32)
        return cotangent / (1.0 + jnp.exp(slope * table + shift))

    row = lax.broadcasted_iota(jnp.int32, (rows, rows), 0)
    paired = (row == match_ref[...]).astype(jnp.float32)
    turned = paired.T
    is_a = (kind == 0).astype(jnp.float32)
    positive = is_a * turned + (1.0 - is_a) * paired
    first = (gradient(own[1], own[0]) - cotangent * positive).astype(jnp.bfloat16)
    total[kind] = jnp.dot(first, own[0], preferred_element_type=jnp.float32)
    total[1 - kind] = lax.dot_general(first, own[1], (((0,), (0,)), ((), ())), preferred_element_type=jnp.float32)

    half = rows // 2

    def work(which, block, start, size):
        other = held[block, pl.ds(start, size)]
        grads = gradient(own[1 - which], other).astype(jnp.bfloat16)
        output = which * (1 - kind) + (1 - which) * kind
        total[output] += jnp.dot(grads, other, preferred_element_type=jnp.float32)

    arrived("sib", 0, PIECES)
    work(1 - logical, SLOT["sib"], 0, rows)

    steps = []
    for c in (0, 1):
        waited, list_c, events = set(), [], []
        for item in PLAN[c]:
            if item[0] == SEND:
                events.append((item[1:], None, []))
                continue
            if item[0] not in (T, H, D):
                name, j = item
                events.append((name, j, FORWARD[c][name](j)))
                waited.add((name, j))
                continue
            halves = [(item[1], 0), (item[1], 1)] if item[0] == T else []
            for n in range(1, len(item) - 1, 2):
                halves.append((item[n], item[n + 1]))
            for name, h in halves:
                for j in range(h * PIECES // 2, (h + 1) * PIECES // 2):
                    if (name, j) not in waited:
                        assert name not in FORWARD[c]
                        events.append((name, j, []))
                        waited.add((name, j))
            fields = [events, (H, T, D).index(item[0])]
            for name, h in (halves[0], halves[-1]):
                fields += [SLOT[name], 0 if name[0] == "a" else 1, h]
            list_c.append(fields)
            events = []
        missing = {(name, j) for name in NAMES for j in range(PIECES)} - waited
        assert not events and {name for name, _ in missing} == {"sib", "b4" if c == 0 else "a4"} - {n for n, _ in waited}
        steps.append(list_c)
    count = max(len(list_c) for list_c in steps)

    def lookup(k, field, default):
        values = []
        for list_c in steps:
            value = jnp.int32(default)
            for n in range(len(list_c)):
                value = jnp.where(k == n, int(list_c[n][field]), value)
            values.append(value)
        return jnp.where(logical == 0, values[0], values[1])

    def branch(k, low, high, run):
        if high - low == 1:
            run(low)
            return
        middle = (low + high) // 2

        @pl.when(k < middle)
        def _():
            branch(k, low, middle, run)

        @pl.when(k >= middle)
        def _():
            branch(k, middle, high, run)

    def take(c, n):
        for name, j, targets in steps[c][n][0]:
            if j is None:
                send_own(c, name)
                continue
            arrived(name, j)
            for where, target in targets:
                send(c, (held, SLOT[name]), where, target, j)

    @pl.loop(0, count)
    def _(k):
        for c in (0, 1):

            @pl.when((logical == c) & (k < len(steps[c])))
            def _(c=c):
                branch(k, 0, len(steps[c]), functools.partial(take, c))

        form = lookup(k, 1, 3)
        block, which, start = lookup(k, 2, 0), lookup(k, 3, 0), lookup(k, 4, 0) * half

        @pl.when(form == 1)
        def _():
            work(which, block, 0, rows)

        @pl.when(form == 0)
        def _():
            work(which, block, pl.multiple_of(start, half), half)

        @pl.when(form == 2)
        def _():
            second = lookup(k, 5, 0), lookup(k, 6, 0), lookup(k, 7, 0) * half
            pair = []
            for block_, which_, start_ in ((block, which, start), second):
                other = held[block_, pl.ds(pl.multiple_of(start_, half), half)]
                pair.append((which_, other, gradient(own[1 - which_], other).astype(jnp.bfloat16)))
            for which_, other, grads in pair:
                output = which_ * (1 - kind) + (1 - which_) * kind
                total[output] += jnp.dot(grads, other, preferred_element_type=jnp.float32)

    for c in (0, 1):

        @pl.when(logical == c)
        def _(c=c):
            for copy in sent[c]:
                copy().wait_send()


def per_device(pictures, captions, matched, multiplier, offset, cotangent):
    rows, width = pictures.shape
    scalars = jnp.stack([multiplier, offset, cotangent])
    matched, pictures, captions = (pltpu.with_memory_space_constraint(v, pltpu.HBM) for v in (matched, pictures, captions))
    sums = pl.pallas_call(
        functools.partial(kernel, rows),
        out_shape=jax.ShapeDtypeStruct((2, rows, width), jnp.float32),
        in_specs=[
            pl.BlockSpec(memory_space=pltpu.SMEM),
            pl.BlockSpec(memory_space=pltpu.HBM),
            pl.BlockSpec(memory_space=pltpu.HBM),
            pl.BlockSpec(memory_space=pltpu.HBM),
        ],
        out_specs=pl.BlockSpec(memory_space=pltpu.VMEM),
        scratch_shapes=[
            pltpu.VMEM((2, rows, width), jnp.bfloat16),
            pltpu.VMEM((len(NAMES), rows, width), jnp.bfloat16),
            pltpu.VMEM((1, rows), jnp.int32),
            pltpu.SemaphoreType.DMA((3,)),
            pltpu.SemaphoreType.DMA((160,)),
            pltpu.SemaphoreType.DMA((len(NAMES), PIECES)),
        ],
        compiler_params=pltpu.CompilerParams(
            collective_id=0, has_side_effects=True, vmem_limit_bytes=LIMIT * 2**20
        ),
        cost_estimate=pl.CostEstimate(
            flops=31 * 2 * rows * rows * width, bytes_accessed=12 * rows * width, transcendentals=16 * rows * rows
        ),
        name="band",
    )(scalars, matched, pictures, captions)
    return multiplier * sums[0], multiplier * sums[1]


def solution(mesh):
    placed = (P("dp", None), P("dp", None), P("dp", None), P(), P(), P())
    return jax.shard_map(
        per_device,
        mesh=mesh,
        in_specs=placed,
        out_specs=(P("dp", None), P("dp", None)),
        check_vma=False,
    )
```

```python
import functools

import jax
import jax.numpy as jnp
from jax import lax
from jax.experimental import pallas as pl
from jax.experimental.pallas import tpu as pltpu
from jax.sharding import PartitionSpec as P

MESH = pl.DeviceIdType.MESH
PIECES = 8
SPLIT = 5
LIMIT = 36

NAMES = (
    "sib", "b1_0", "b1_1", "a2_0", "a2_1", "b2_0", "b2_1", "a1_0", "a1_1",
    "b3_0", "b3_1", "a3_0", "a3_1", "a4", "b4",
)
SLOT = {name: i for i, name in enumerate(NAMES)}

FORWARD = (
    {
        "a2_0": lambda j: [("X", "b3_1"), ("S", "a2_0")] if j < SPLIT else [("S", "a2_0")],
        "b1_0": lambda j: [("S", "b1_0")],
        "b2_0": lambda j: [("X", "a1_1"), ("P", "b4"), ("S", "b2_0")],
        "a1_0": lambda j: [("N", "a3_0"), ("S", "a1_0")],
        "b3_0": lambda j: [("S", "b3_0")],
        "b4": lambda j: [("X", "a3_1"), ("S", "b4")],
        "a3_0": lambda j: [("S", "a3_0")],
    },
    {
        "a2_1": lambda j: [("X", "b3_0"), ("N0", "a4"), ("S", "a2_1")],
        "b1_1": lambda j: [("P", "b3_1"), ("S", "b1_1")] if j >= SPLIT else [("S", "b1_1")],
        "b2_1": lambda j: [("X", "a1_0"), ("S", "b2_1")],
        "a1_1": lambda j: [("S", "a1_1")],
        "b3_1": lambda j: [("X", "a2_0"), ("S", "b3_1")] if j >= SPLIT else [("S", "b3_1")],
        "a3_1": lambda j: [("S", "a3_1")],
    },
)

sib, b1_0, b1_1, a2_0, a2_1, b2_0, b2_1, a1_0, a1_1, b3_0, b3_1, a3_0, a3_1, a4, b4 = NAMES
T, H, D, SEND, N, P_, X = "T", "H", "D", ">", "N", "P", "X"

OWN = (
    [
        (N, a2_0, 0), (X, b1_1, 4), (X, b1_1, 6), (P_, b2_0, 0), (X, b1_1, 7), (X, b1_1, 1), (X, b1_1, 3),
        (N, a2_0, 2), (P_, b2_0, 6),
    ],
    [
        (P_, b2_1, 3), (N, a2_1, 4), (X, b1_0, 6), (P_, b2_1, 4),
    ],
)

PLAN = (
    [
        (SEND, P_, b2_0, 4), (SEND, X, b1_1, 2), (SEND, N, a2_0, 4), (SEND, P_, b2_0, 3), (SEND, X, b1_1, 0),
        (SEND, X, b1_1, 5), (SEND, P_, b2_0, 5), (SEND, N, a2_0, 1), (b1_0, 0), (a2_0, 0), (SEND, P_, b2_0, 1),
        (b1_0, 6), (SEND, N, a2_0, 3), (SEND, P_, b2_0, 7), (a2_0, 1), (b1_0, 4), (a1_0, 3),
        (SEND, P_, b2_0, 2), (T, b1_1), (b1_0, 5), (b1_0, 7), (H, b1_0, 1), (b3_0, 6), (b1_0, 3), (a2_0, 2),
        (b3_0, 0), (a1_0, 1), (H, a2_1, 0), (a2_0, 4), (b1_0, 2), (a1_0, 4), (b2_0, 4), (b2_0, 0), (b2_0, 1),
        (b2_0, 2), (b2_0, 3), (D, a2_1, 1, b2_0, 0), (b2_0, 5), (b2_0, 6), (b2_0, 7), (H, b2_0, 1), (b3_0, 1),
        (b3_0, 2), (b3_0, 3), (b3_0, 4), (b3_0, 5), (b3_0, 7), (T, b3_0), (b1_0, 1), (a2_0, 3), (T, b2_1),
        (a1_0, 0), (b4, 0), (H, b1_0, 0), (a1_0, 2), (a1_0, 5), (a1_0, 6), (a1_0, 7), (T, a1_0), (H, b3_1, 1),
        (b4, 1), (H, b3_1, 0), (b4, 2), (b4, 5), (b4, 3), (a2_0, 7), (b4, 4), (a2_0, 6), (a3_0, 1), (a2_0, 5),
        (T, a2_0), (a3_0, 4), (b4, 6), (a3_0, 0), (b4, 7), (a3_0, 2), (T, a1_1), (a3_0, 5), (a3_0, 3),
        (D, a4, 1, a3_0, 0), (a3_0, 6), (a3_0, 7), (D, a4, 0, a3_0, 1), (T, a3_1),
    ],
    [
        (SEND, X, b1_0, 0), (SEND, X, b1_0, 7), (SEND, P_, b2_1, 5), (SEND, N, a2_1, 3), (SEND, X, b1_0, 4),
        (SEND, X, b1_0, 1), (b1_1, 3), (SEND, N, a2_1, 1), (SEND, P_, b2_1, 2), (SEND, N, a2_1, 6),
        (SEND, X, b1_0, 3), (SEND, N, a2_1, 0), (SEND, N, a2_1, 5), (SEND, P_, b2_1, 1), (b1_1, 4),
        (SEND, X, b1_0, 2), (SEND, P_, b2_1, 6), (SEND, X, b1_0, 5), (SEND, P_, b2_1, 0), (b2_1, 5), (b1_1, 6),
        (b2_1, 2), (SEND, P_, b2_1, 7), (b1_1, 0), (b1_1, 5), (SEND, N, a2_1, 2), (b2_1, 4), (SEND, N, a2_1, 7),
        (b1_1, 7), (b2_1, 3), (a2_1, 6), (b1_1, 1), (b1_1, 2), (T, b1_1), (b2_1, 1), (a2_1, 1), (a2_1, 0),
        (a2_1, 2), (a2_1, 3), (a2_1, 4), (a2_1, 5), (a2_1, 7), (T, a2_1), (b2_1, 0), (b2_1, 6), (b2_1, 7),
        (T, b2_1), (T, b2_0), (H, b1_0, 0), (H, b1_0, 1), (a1_1, 0), (b3_1, 6), (b3_1, 4), (b3_1, 2), (b3_1, 5),
        (b3_1, 7), (D, b3_1, 1, b3_0, 0), (a1_1, 3), (b3_1, 0), (b3_1, 1), (b3_1, 3), (D, b3_1, 0, b3_0, 1),
        (a1_1, 1), (a1_1, 2), (a1_1, 4), (a1_1, 5), (a1_1, 6), (a1_1, 7), (T, a1_1), (T, a1_0), (T, a2_0),
        (T, b4), (a3_1, 2), (a3_1, 6), (a3_1, 5), (a3_1, 0), (a3_1, 1), (a3_1, 3), (a3_1, 4), (a3_1, 7),
        (T, a3_1), (T, a3_0),
    ],
)


def coordinates():
    shard, replica = lax.axis_index("dp"), lax.axis_index("rep")
    return shard // 16, (shard // 4) % 4, replica * 2 + (shard // 2) % 2, shard % 2


def device(z, y, x, core):
    return (z * 16 + y * 4 + (x % 2) * 2 + core, x // 2)


def kernel(
    rows, scalars, match_hbm, picture_hbm, caption_hbm, total,
    own, held, match_ref, load_sem, send_sem, recv_sem,
):
    z, y, x, core = coordinates()
    kind = x % 2
    logical = (core + kind) % 2
    part = rows // PIECES
    up = ((z + (y + 1) // 4) % 8, (y + 1) % 4)
    down = ((z + 7 + (y + 3) // 4) % 8, (y + 3) % 4)
    next_z, next_y = [u * (1 - kind) + d * kind for u, d in zip(up, down)]
    prev_z, prev_y = [d * (1 - kind) + u * kind for u, d in zip(up, down)]
    place = {
        "S": device(z, y, x, 1 - core),
        "N": device(next_z, next_y, x, core),
        "P": device(prev_z, prev_y, x, core),
        "N0": device(next_z, next_y, x, kind),
        "P1": device(prev_z, prev_y, x, 1 - kind),
        "R": device(z, y, (x + 1) % 4, core),
        "L": device(z, y, (x + 3) % 4, core),
    }

    loads = [
        pltpu.make_async_copy(picture_hbm, own.at[1 - kind], load_sem.at[0]),
        pltpu.make_async_copy(caption_hbm, own.at[kind], load_sem.at[1]),
        pltpu.make_async_copy(match_hbm, match_ref, load_sem.at[2]),
    ]
    for load in loads:
        load.start()

    barrier = pltpu.get_barrier_semaphore()
    for where in "SNPRL":
        pl.semaphore_signal(barrier, inc=1, device_id=place[where], device_id_type=MESH)

    @pl.when(logical == 0)
    def _():
        pl.semaphore_signal(barrier, inc=1, device_id=place["P1"], device_id_type=MESH)
        pl.semaphore_wait(barrier, 5)

    @pl.when(logical == 1)
    def _():
        pl.semaphore_wait(barrier, 6)

    for load in loads:
        load.wait()

    sent = ([], [])

    def piece(ref, block, j, count=1):
        return ref.at[block, pl.ds(j * part, count * part)]

    def send(c, src, where, name, j, count=1):
        if where == "X":
            where = "RL"[j % 2]
        index = len(sent[c])

        def copy():
            return pltpu.make_async_remote_copy(
                src_ref=piece(src[0], src[1], j, count),
                dst_ref=piece(held, SLOT[name], j, count),
                send_sem=send_sem.at[index],
                recv_sem=recv_sem.at[SLOT[name], j],
                device_id=place[where],
                device_id_type=MESH,
            )

        copy().start()
        sent[c].append(copy)

    def arrived(name, j, count=1):
        here = piece(held, SLOT[name], j, count)
        pltpu.make_async_remote_copy(
            src_ref=here, dst_ref=here, send_sem=send_sem.at[0], recv_sem=recv_sem.at[SLOT[name], j],
            device_id=place["S"], device_id_type=MESH,
        ).wait_recv()

    def send_own(c, item):
        where, name, j = item
        send(c, (own, 1 if where == "P" else 0), where, name, j)

    for c in (0, 1):

        @pl.when(logical == c)
        def _(c=c):
            send(c, (own, c), "S", "sib", 0, PIECES)
            for item in OWN[c]:
                send_own(c, item)

    multiplier, offset, cotangent = scalars[0], scalars[1], scalars[2]
    slope, shift = -multiplier, -offset

    def gradient(left, right):
        table = lax.dot_general(left, right, (((1,), (1,)), ((), ())), preferred_element_type=jnp.float32)
        return cotangent / (1.0 + jnp.exp(slope * table + shift))

    row = lax.broadcasted_iota(jnp.int32, (rows, rows), 0)
    paired = (row == match_ref[...]).astype(jnp.float32)
    turned = paired.T
    is_a = (kind == 0).astype(jnp.float32)
    positive = is_a * turned + (1.0 - is_a) * paired
    first = (gradient(own[1], own[0]) - cotangent * positive).astype(jnp.bfloat16)
    total[kind] = jnp.dot(first, own[0], preferred_element_type=jnp.float32)
    total[1 - kind] = lax.dot_general(first, own[1], (((0,), (0,)), ((), ())), preferred_element_type=jnp.float32)

    half = rows // 2

    def work(which, block, start, size):
        other = held[block, pl.ds(start, size)]
        grads = gradient(own[1 - which], other).astype(jnp.bfloat16)
        output = which * (1 - kind) + (1 - which) * kind
        total[output] += jnp.dot(grads, other, preferred_element_type=jnp.float32)

    arrived("sib", 0, PIECES)
    work(1 - logical, SLOT["sib"], 0, rows)

    steps = []
    for c in (0, 1):
        waited, list_c, events = set(), [], []
        for item in PLAN[c]:
            if item[0] == SEND:
                events.append((item[1:], None, []))
                continue
            if item[0] not in (T, H, D):
                name, j = item
                events.append((name, j, FORWARD[c][name](j)))
                waited.add((name, j))
                continue
            halves = [(item[1], 0), (item[1], 1)] if item[0] == T else []
            for n in range(1, len(item) - 1, 2):
                halves.append((item[n], item[n + 1]))
            for name, h in halves:
                for j in range(h * PIECES // 2, (h + 1) * PIECES // 2):
                    if (name, j) not in waited:
                        assert name not in FORWARD[c]
                        events.append((name, j, []))
                        waited.add((name, j))
            fields = [events, (H, T, D).index(item[0])]
            for name, h in (halves[0], halves[-1]):
                fields += [SLOT[name], 0 if name[0] == "a" else 1, h]
            list_c.append(fields)
            events = []
        missing = {(name, j) for name in NAMES for j in range(PIECES)} - waited
        assert not events and {name for name, _ in missing} == {"sib", "b4" if c == 0 else "a4"} - {n for n, _ in waited}
        steps.append(list_c)
    count = max(len(list_c) for list_c in steps)

    def lookup(k, field, default):
        values = []
        for list_c in steps:
            value = jnp.int32(default)
            for n in range(len(list_c)):
                value = jnp.where(k == n, int(list_c[n][field]), value)
            values.append(value)
        return jnp.where(logical == 0, values[0], values[1])

    def branch(k, low, high, run):
        if high - low == 1:
            run(low)
            return
        middle = (low + high) // 2

        @pl.when(k < middle)
        def _():
            branch(k, low, middle, run)

        @pl.when(k >= middle)
        def _():
            branch(k, middle, high, run)

    def take(c, n):
        for name, j, targets in steps[c][n][0]:
            if j is None:
                send_own(c, name)
                continue
            arrived(name, j)
            for where, target in targets:
                send(c, (held, SLOT[name]), where, target, j)

    @pl.loop(0, count)
    def _(k):
        for c in (0, 1):

            @pl.when((logical == c) & (k < len(steps[c])))
            def _(c=c):
                branch(k, 0, len(steps[c]), functools.partial(take, c))

        form = lookup(k, 1, 3)
        block, which, start = lookup(k, 2, 0), lookup(k, 3, 0), lookup(k, 4, 0) * half

        @pl.when(form == 1)
        def _():
            work(which, block, 0, rows)

        @pl.when(form == 0)
        def _():
            work(which, block, pl.multiple_of(start, half), half)

        @pl.when(form == 2)
        def _():
            second = lookup(k, 5, 0), lookup(k, 6, 0), lookup(k, 7, 0) * half
            pair = []
            for block_, which_, start_ in ((block, which, start), second):
                other = held[block_, pl.ds(pl.multiple_of(start_, half), half)]
                pair.append((which_, other, gradient(own[1 - which_], other).astype(jnp.bfloat16)))
            for which_, other, grads in pair:
                output = which_ * (1 - kind) + (1 - which_) * kind
                total[output] += jnp.dot(grads, other, preferred_element_type=jnp.float32)

    for c in (0, 1):

        @pl.when(logical == c)
        def _(c=c):
            for copy in sent[c]:
                copy().wait_send()


def per_device(pictures, captions, matched, multiplier, offset, cotangent):
    rows, width = pictures.shape
    scalars = jnp.stack([multiplier, offset, cotangent])
    matched, pictures, captions = (pltpu.with_memory_space_constraint(v, pltpu.HBM) for v in (matched, pictures, captions))
    sums = pl.pallas_call(
        functools.partial(kernel, rows),
        out_shape=jax.ShapeDtypeStruct((2, rows, width), jnp.float32),
        in_specs=[
            pl.BlockSpec(memory_space=pltpu.SMEM),
            pl.BlockSpec(memory_space=pltpu.HBM),
            pl.BlockSpec(memory_space=pltpu.HBM),
            pl.BlockSpec(memory_space=pltpu.HBM),
        ],
        out_specs=pl.BlockSpec(memory_space=pltpu.VMEM),
        scratch_shapes=[
            pltpu.VMEM((2, rows, width), jnp.bfloat16),
            pltpu.VMEM((len(NAMES), rows, width), jnp.bfloat16),
            pltpu.VMEM((1, rows), jnp.int32),
            pltpu.SemaphoreType.DMA((3,)),
            pltpu.SemaphoreType.DMA((160,)),
            pltpu.SemaphoreType.DMA((len(NAMES), PIECES)),
        ],
        compiler_params=pltpu.CompilerParams(
            collective_id=0, has_side_effects=True, vmem_limit_bytes=LIMIT * 2**20
        ),
        cost_estimate=pl.CostEstimate(
            flops=31 * 2 * rows * rows * width, bytes_accessed=12 * rows * width, transcendentals=16 * rows * rows
        ),
        name="band",
    )(scalars, matched, pictures, captions)
    return multiplier * sums[0], multiplier * sums[1]


def solution(mesh):
    placed = (P("dp", None), P("dp", None), P("dp", None), P(), P(), P())
    return jax.shard_map(
        per_device,
        mesh=mesh,
        in_specs=placed,
        out_specs=(P("dp", None), P("dp", None)),
        check_vma=False,
    )
```
